32 devices in a mesh: samp: 8 (over z, y), var: 4 (over x, core).
Axes of the slice: x: 2, y: 2, z: 4, core: 2. Of those that a mesh axis runs over, the one named last changes fastest.
Arguments:
- genotypes: int32 [2048, 4096], P('samp', 'var'), may hold values from -1 to 2, as said below
- ancestry: float32 [16, 2048], P(None, 'samp'), may hold values from 0.05 to 4, as said below
- frequency: float32 [16, 4096], P(None, 'var'), may hold values from 0.05 to 0.95
Outputs:
- new_ancestry: float32 [16, 2048], P(None, 'samp')
- new_frequency: float32 [16, 4096], P(None, 'var')
The draws below stay inside these ranges and needn't reach their ends.
Inputs may be any that keep to these rules, and one draw needn't show every extreme that they name: `genotypes`: A dosage of 0, 1 or 2 alternate alleles, or -1 for a missing genotype. `ancestry`: positive weights.
All inputs are finite; a program needn't handle non-finite values.
Results may differ from the reference program's by a relative error of at most 0.0003.
Values sent between devices are 32-bit elements; how exact they have to be, the bound alone decides.
A program may use at most 64 MiB of HBM per device.

```python
import jax
import jax.numpy as jnp
from jax import lax

K = 16
COLS_DEV = 1024
ITERS = 4
NIND = 2048
NVAR = 4096


def population_plan(key):
    base = jax.random.fold_in(key, 7)
    key_order, key_second, key_mixing = jax.random.split(base, 3)
    order = jax.random.permutation(key_order, jnp.arange(K, dtype=jnp.int32))
    block_index = jnp.arange(NIND, dtype=jnp.int32) * K // NIND
    first_parent = jnp.take(order, block_index)
    second_parent = jax.random.randint(key_second, (NIND,), 0, K, dtype=jnp.int32)
    mixing = jax.random.randint(key_mixing, (NIND, 1), 2, 5, dtype=jnp.int32)
    return (first_parent, second_parent, mixing)


def draw_genotypes(key, part):
    first_parent, second_parent, mixing = population_plan(key)
    level_key = jax.random.fold_in(key, 11)
    key_low, key_high, key_pick, key_random = jax.random.split(level_key, 4)
    low_levels = jax.random.randint(key_low, (K, NVAR), 1, 5, dtype=jnp.int32)
    high_levels = jax.random.randint(key_high, (K, NVAR), 60, 64, dtype=jnp.int32)
    picks = jax.random.randint(key_pick, (K, NVAR), 0, 2, dtype=jnp.int32)
    levels = jnp.where(picks == 1, high_levels, low_levels)
    first_level = jnp.take(levels, first_parent, axis=0)
    second_level = jnp.take(levels, second_parent, axis=0)
    random_bits = jax.random.randint(key_random, (NIND, NVAR), 0, 2 ** 30, dtype=jnp.int32)
    level_one = jnp.where(random_bits % 4 < mixing, first_level, second_level)
    level_two = jnp.where(random_bits // 4 % 4 < mixing, first_level, second_level)
    allele_one = (random_bits // 16 % 64 < level_one).astype(jnp.int32)
    allele_two = (random_bits // 1024 % 64 < level_two).astype(jnp.int32)
    missing = random_bits // 65536 % 32 == 0
    return jnp.where(missing, jnp.int32(-1), allele_one + allele_two)


def draw_ancestry(key, part):
    first_parent, second_parent, mixing = population_plan(key)
    rows = jnp.arange(K, dtype=jnp.int32)[:, None]
    member = (rows == first_parent[None, :]).astype(jnp.float32)
    noise_key = jax.random.fold_in(key, 13)
    noise = jnp.exp(jax.random.uniform(noise_key, (K, NIND), jnp.float32, jnp.log(0.1), 0.0))
    boost = 2.0
    return (noise * (1.0 + boost * member)).astype(jnp.float32)


def shard_levels(own_key, extent, cuts, low, top_value):
    loudness = 1.0
    for dim, blocks in cuts:
        heights = jax.random.uniform(jax.random.fold_in(jax.random.fold_in(own_key, 6), dim), (blocks,), jnp.float32, low / len(cuts), top_value / len(cuts))
        loudness = loudness * jnp.repeat(jnp.exp(heights), extent[dim] // blocks).reshape((-1,) + (1,) * (len(extent) - 1 - dim))
    return loudness


def setup_inputs(seed: int = 0) -> dict:
    splits = jax.random.split(jax.random.key(seed), 4)
    genotypes = draw_genotypes(jax.random.fold_in(splits[3], 71), 0)
    ancestry = draw_ancestry(jax.random.fold_in(splits[3], 71), 0)
    frequency = jnp.clip(0.05 + 0.9 * jax.random.uniform(splits[2], (K, NVAR), jnp.float32) ** shard_levels(splits[2], (K, NVAR), ((1, 4),), -0.2, 0.2), 0.05, 0.95)
    return dict(genotypes=genotypes, ancestry=ancestry, frequency=frequency)


HIGH = lax.Precision.HIGHEST


def ratios(block, expected):
    present = (block >= 0).astype(jnp.float32)
    dosage = jnp.maximum(block, 0).astype(jnp.float32)
    return present * dosage / expected, present * (2.0 - dosage) / (1.0 - expected)


def contract(left, right, left_dim, right_dim):
    return lax.dot_general(left, right, (((left_dim,), (right_dim,)), ((), ())), precision=HIGH, preferred_element_type=jnp.float32)


def reference(genotypes, ancestry, frequency):
    fraction = ancestry / jnp.sum(ancestry, axis=0, keepdims=True)
    blocks = NVAR // COLS_DEV
    starts = jnp.arange(blocks, dtype=jnp.int32) * COLS_DEV
    for sweep in range(ITERS):
        def q_part(total, start):
            block = lax.dynamic_slice_in_dim(genotypes, start, COLS_DEV, 1)
            freq_block = lax.dynamic_slice_in_dim(frequency, start, COLS_DEV, 1)
            expected = contract(fraction, freq_block, 0, 0)
            ratio_ref, ratio_alt = ratios(block, expected)
            term = contract(freq_block, ratio_ref, 1, 1) + contract(1.0 - freq_block, ratio_alt, 1, 1)
            return total + term, None

        total, unused = lax.scan(q_part, jnp.zeros((K, NIND), jnp.float32), starts)
        weighted = fraction * total
        fraction = weighted / jnp.sum(weighted, axis=0, keepdims=True)

        def p_part(start):
            block = lax.dynamic_slice_in_dim(genotypes, start, COLS_DEV, 1)
            freq_block = lax.dynamic_slice_in_dim(frequency, start, COLS_DEV, 1)
            expected = contract(fraction, freq_block, 0, 0)
            ratio_ref, ratio_alt = ratios(block, expected)
            upper = freq_block * contract(fraction, ratio_ref, 1, 0)
            lower = (1.0 - freq_block) * contract(fraction, ratio_alt, 1, 0)
            return upper / (upper + lower)

        updated = lax.map(p_part, starts)
        frequency = jnp.transpose(updated, (1, 0, 2)).reshape(K, NVAR)
    return fraction, frequency
```

```python
import functools

import jax
import jax.numpy as jnp
from jax import lax
from jax.experimental import pallas as pl
from jax.experimental.pallas import tpu as pltpu
from jax.sharding import PartitionSpec as P

ITERS = 4
MESH = pl.DeviceIdType.MESH
BF = jnp.bfloat16
F32 = jnp.float32


def rounded(x):
    return x.astype(BF).astype(F32)


def split3(x):
    x1 = rounded(x)
    rest = x - x1
    x2 = rounded(rest)
    x3 = rounded(rest - x2)
    return x1, x2, x3


def split2(x):
    hi = x.astype(BF)
    return hi, (x - hi.astype(F32)).astype(BF)


def dot(left, right, right_dim):
    return lax.dot_general(
        left, right, (((1,), (right_dim,)), ((), ())), preferred_element_type=F32
    )


def kernel(
    S, V, C, W, G,
    geno, anc, freq0, out_f, out_p,
    a_ref, b_ref, pcat, fbuf, qbuf, psrc, precv,
    q_send, q_recv, p_send, p_recv, g_send, g_recv,
):
    K, rows = anc.shape
    pairs = C // G
    width = W * G
    samp = lax.axis_index("samp")
    var = lax.axis_index("var")
    owner_only = S != C

    barrier = pltpu.get_barrier_semaphore()
    for d in range(1, S):
        pl.semaphore_signal(
            barrier, inc=1, device_id=(lax.rem(samp + d, S), var), device_id_type=MESH
        )
    for d in range(1, V):
        pl.semaphore_signal(
            barrier, inc=1, device_id=(samp, lax.rem(var + d, V)), device_id_type=MESH
        )

    def q_copy(s, slot, peer):
        return pltpu.make_async_remote_copy(
            src_ref=qbuf.at[s, slot], dst_ref=qbuf.at[s, slot],
            send_sem=q_send.at[s, peer], recv_sem=q_recv.at[s, slot],
            device_id=(samp, peer), device_id_type=MESH,
        )

    def p_copy(s, j, slot, peer):
        return pltpu.make_async_remote_copy(
            src_ref=psrc.at[s, j], dst_ref=precv.at[s, slot],
            send_sem=p_send.at[s, j], recv_sem=p_recv.at[s, slot],
            device_id=(peer, var), device_id_type=MESH,
        )

    def g_copy(s, slot, peer):
        return pltpu.make_async_remote_copy(
            src_ref=fbuf.at[s + 1, slot], dst_ref=fbuf.at[s + 1, slot],
            send_sem=g_send.at[s, peer], recv_sem=g_recv.at[s, slot],
            device_id=(peer, var), device_id_type=MESH,
        )

    def when_owner(f):
        if owner_only:
            pl.when(samp < C)(f)
        else:
            f()

    def columns(pair):
        return pl.ds(pl.multiple_of(pair * width, width), width)

    def prepare(pair):
        g = geno[:, columns(pair)]
        present = g >= 0
        a_ref[:, columns(pair)] = jnp.maximum(g, 0).astype(F32)
        b_ref[:, columns(pair)] = jnp.where(present, 2.0, 0.0)

    def fraction_rows(f):
        f1, f2, f3 = split3(f)
        stacked = jnp.concatenate([f1, f1, f2, f2, f1, f3, f2, f3], axis=0)
        return jnp.transpose(stacked).astype(BF)

    def frequency_of(s, pair):
        return jnp.concatenate([fbuf[s, pair * G + i] for i in range(G)], axis=1)

    own_pair = lax.rem(samp, C) // G

    for j in range(C):
        fbuf[0, j] = freq0[:, j * W:(j + 1) * W]
    f = anc[...]
    f = f / jnp.sum(f, axis=0, keepdims=True)
    count = None
    for s in range(ITERS):
        f_t = fraction_rows(f)
        total = jnp.zeros((2 * K, rows), F32)
        present_sum = jnp.zeros((8, rows), F32)
        for step in range(pairs):
            pair = lax.rem(own_pair + step, pairs)
            if s == 0:
                prepare(pair)
            else:
                for i in range(G):
                    j = pair * G + i

                    @pl.when(j != samp)
                    def _():
                        g_copy(s - 1, j, j).wait_recv()
            p1, p2, p3 = split3(frequency_of(s, pair))
            cat = jnp.concatenate([p1, p2, p1, p2, p3, p1, p3, p2], axis=0).astype(BF)
            pcat[pair] = cat
            e = dot(f_t, cat, 0)
            a = a_ref[:, columns(pair)]
            b = b_ref[:, columns(pair)]
            diff = (a - b * e) * pl.reciprocal(e * (1.0 - e))
            hi, lo = split2(diff)
            left = cat[: 2 * K]
            total = total + dot(left, hi, 1) + dot(left, lo, 1)
            if s == 0:
                present_sum = present_sum + dot(jnp.ones((8, width), BF), b.astype(BF), 1)
        mine = total[:K] + total[K:]
        qbuf[s, var, :K] = mine
        if s == 0:
            qbuf[s, var, K:] = present_sum
            pl.semaphore_wait(barrier, S - 1 + V - 1)
        for d in range(1, V):
            q_copy(s, var, lax.rem(var + d, V)).start()
        for d in range(1, V):
            peer = lax.rem(var + d, V)
            q_copy(s, peer, peer).wait_recv()
        big = qbuf[s, 0, :K]
        for v in range(1, V):
            big = big + qbuf[s, v, :K]
        if s == 0:
            count = qbuf[0, 0, K:K + 8]
            for v in range(1, V):
                count = count + qbuf[0, v, K:K + 8]
            count = 1.0 / count[:1]
        mean = jnp.sum(f * big, axis=0, keepdims=True)
        f = f + f * ((big - mean) * count)

        f_t = fraction_rows(f)
        f_hi, f_lo = split2(f)
        left = jnp.concatenate([f_hi, f_lo], axis=0)
        for step in range(pairs):
            pair = lax.rem(own_pair + 1 + step, pairs)
            e = dot(f_t, pcat[pair], 0)
            a = a_ref[:, columns(pair)]
            b = b_ref[:, columns(pair)]
            om = 1.0 - e
            inv = pl.reciprocal(e * om)
            ref_hi, ref_lo = split2(a * (om * inv))
            alt_hi, alt_lo = split2((b - a) * (e * inv))
            up = dot(left, ref_hi, 0) + dot(left, ref_lo, 0)
            low = dot(left, alt_hi, 0) + dot(left, alt_lo, 0)
            both = jnp.concatenate([up[:K] + up[K:], low[:K] + low[K:]], axis=0)
            for i in range(G):
                j = pair * G + i
                part = both[:, i * W:(i + 1) * W]
                psrc[s, j] = part

                @pl.when(j == samp)
                def _():
                    precv[s, samp] = part

                @pl.when(j != samp)
                def _():
                    p_copy(s, j, samp, j).start()

        @when_owner
        def _():
            for d in range(1, S):
                peer = lax.rem(samp + d, S)
                p_copy(s, 0, peer, peer).wait_recv()
            sums = precv[s, 0]
            for q in range(1, S):
                sums = sums + precv[s, q]
            old = fbuf[s, samp]
            upper = old * sums[:K]
            lower = (1.0 - old) * sums[K:]
            fbuf[s + 1, samp] = upper / (upper + lower)
            for d in range(1, S):
                g_copy(s, samp, lax.rem(samp + d, S)).start()

    out_f[...] = f
    for j in range(C):
        @pl.when(j != samp)
        def _():
            g_copy(ITERS - 1, j, j).wait_recv()
        out_p[:, j * W:(j + 1) * W] = fbuf[ITERS, j]

    for s in range(ITERS):
        for d in range(1, V):
            q_copy(s, var, lax.rem(var + d, V)).wait_send()
        for j in range(C):
            @pl.when(j != samp)
            def _():
                p_copy(s, j, samp, j).wait_send()

        @when_owner
        def _():
            for d in range(1, S):
                g_copy(s, samp, lax.rem(samp + d, S)).wait_send()


def shards(S, V, genotypes, ancestry, frequency):
    rows, cols = genotypes.shape
    K = ancestry.shape[0]
    W = max(128, cols // S)
    C = cols // W
    G = 2 if W == 128 and C % 2 == 0 else 1
    dma = pltpu.SemaphoreType.DMA
    vmem = pl.BlockSpec(memory_space=pltpu.VMEM)
    return pl.pallas_call(
        functools.partial(kernel, S, V, C, W, G),
        out_shape=(
            jax.ShapeDtypeStruct(ancestry.shape, F32),
            jax.ShapeDtypeStruct(frequency.shape, F32),
        ),
        in_specs=[vmem] * 3,
        out_specs=(vmem, vmem),
        scratch_shapes=[
            pltpu.VMEM((rows, cols), F32),
            pltpu.VMEM((rows, cols), F32),
            pltpu.VMEM((C // G, 8 * K, W * G), BF),
            pltpu.VMEM((ITERS + 1, C, K, W), F32),
            pltpu.VMEM((ITERS, V, K + 8, rows), F32),
            pltpu.VMEM((ITERS, C, 2 * K, W), F32),
            pltpu.VMEM((ITERS, S, 2 * K, W), F32),
            dma((ITERS, V)), dma((ITERS, V)),
            dma((ITERS, C)), dma((ITERS, S)),
            dma((ITERS, S)), dma((ITERS, C)),
        ],
        compiler_params=pltpu.CompilerParams(
            collective_id=0, has_side_effects=True, vmem_limit_bytes=40 * 2 ** 20
        ),
        cost_estimate=pl.CostEstimate(
            flops=2 * 4 * 8 * rows * cols * K,
            bytes_accessed=4 * rows * cols,
            transcendentals=8 * rows * cols,
        ),
        name="em_sweeps",
    )(genotypes, ancestry, frequency)


def solution(mesh):
    return jax.shard_map(
        functools.partial(shards, mesh.shape["samp"], mesh.shape["var"]),
        mesh=mesh,
        in_specs=(P("samp", "var"), P(None, "samp"), P(None, "var")),
        out_specs=(P(None, "samp"), P(None, "var")),
        check_vma=False,
    )
```

```python
import functools

import jax
import jax.numpy as jnp
from jax import lax
from jax.experimental import pallas as pl
from jax.experimental.pallas import tpu as pltpu
from jax.sharding import PartitionSpec as P

ITERS = 4
MESH = pl.DeviceIdType.MESH
BF = jnp.bfloat16
F32 = jnp.float32


def rounded(x):
    return x.astype(BF).astype(F32)


def split3(x):
    x1 = rounded(x)
    rest = x - x1
    x2 = rounded(rest)
    x3 = rounded(rest - x2)
    return x1, x2, x3


def split2(x):
    hi = x.astype(BF)
    return hi, (x - hi.astype(F32)).astype(BF)


def dot(left, right, right_dim):
    return lax.dot_general(
        left, right, (((1,), (right_dim,)), ((), ())), preferred_element_type=F32
    )


def kernel(
    S, V, C, W,
    geno_hbm, anc_hbm, freq_hbm, out_f, out_p,
    geno, anc, a_ref, b_ref, pcat, fbuf, qbuf, psrc, precv,
    in_sem, geno_sem, q_send, q_recv, p_send, p_recv, g_send, g_recv,
):
    K, rows = anc.shape
    samp = lax.axis_index("samp")
    var = lax.axis_index("var")
    first = (S - C) // 2
    mine_id = samp - first
    owner = jnp.logical_and(mine_id >= 0, mine_id < C)
    half = C // 2
    side, low_part = samp // (S // 2), lax.rem(samp, half)

    def chunk(step):
        return lax.rem(side + step // half, 2) * half + lax.rem(low_part + step % half, half)

    loads = [pltpu.make_async_copy(anc_hbm, anc, in_sem.at[C])]
    for j in range(C):
        loads.append(
            pltpu.make_async_copy(
                freq_hbm.at[:, pl.ds(j * W, W)], fbuf.at[0, j], in_sem.at[j]
            )
        )
    for load in loads:
        load.start()

    def geno_load(j):
        at = pl.ds(pl.multiple_of(j * W, W), W)
        return pltpu.make_async_copy(geno_hbm.at[:, at], geno.at[j], geno_sem.at[j])

    for step in range(C):
        geno_load(chunk(step)).start()

    barrier = pltpu.get_barrier_semaphore()
    for d in range(1, S):
        pl.semaphore_signal(
            barrier, inc=1, device_id=(lax.rem(samp + d, S), var), device_id_type=MESH
        )
    for d in range(1, V):
        pl.semaphore_signal(
            barrier, inc=1, device_id=(samp, lax.rem(var + d, V)), device_id_type=MESH
        )

    def q_copy(s, slot, peer):
        return pltpu.make_async_remote_copy(
            src_ref=qbuf.at[s, slot], dst_ref=qbuf.at[s, slot],
            send_sem=q_send.at[s, peer], recv_sem=q_recv.at[s, slot],
            device_id=(samp, peer), device_id_type=MESH,
        )

    def p_copy(s, j, slot, peer):
        return pltpu.make_async_remote_copy(
            src_ref=psrc.at[s, j], dst_ref=precv.at[s, slot],
            send_sem=p_send.at[s, j], recv_sem=p_recv.at[s, slot],
            device_id=(peer, var), device_id_type=MESH,
        )

    def g_copy(s, slot, peer):
        return pltpu.make_async_remote_copy(
            src_ref=fbuf.at[s + 1, slot], dst_ref=fbuf.at[s + 1, slot],
            send_sem=g_send.at[s, peer], recv_sem=g_recv.at[s, slot],
            device_id=(peer, var), device_id_type=MESH,
        )

    def prepare(j):
        geno_load(j).wait()
        g = geno[j]
        present = g >= 0
        a_ref[j] = jnp.maximum(g, 0).astype(F32)
        b_ref[j] = jnp.where(present, 2.0, 0.0)

    def fraction_rows(f):
        f1, f2, f3 = split3(f)
        stacked = jnp.concatenate([f1, f1, f2, f2, f1, f3, f2, f3], axis=0)
        return jnp.transpose(stacked).astype(BF)

    for load in loads:
        load.wait()
    f = anc[...]
    f = f / jnp.sum(f, axis=0, keepdims=True)
    count = None
    for s in range(ITERS):
        f_t = fraction_rows(f)
        total = jnp.zeros((2 * K, rows), F32)
        present_sum = jnp.zeros((8, rows), F32)
        for step in range(C):
            j = chunk(step)
            if s == 0:
                prepare(j)
            else:

                @pl.when(j != mine_id)
                def _():
                    g_copy(s - 1, j, j).wait_recv()
            p1, p2, p3 = split3(fbuf[s, j])
            cat = jnp.concatenate([p1, p2, p1, p2, p3, p1, p3, p2], axis=0).astype(BF)
            pcat[j] = cat
            e = dot(f_t, cat, 0)
            a = a_ref[j]
            b = b_ref[j]
            diff = (a - b * e) * pl.reciprocal(e * (1.0 - e))
            hi, lo = split2(diff)
            left = cat[: 2 * K]
            total = total + dot(left, hi, 1) + dot(left, lo, 1)
            if s == 0:
                present_sum = present_sum + dot(jnp.ones((8, W), BF), b.astype(BF), 1)
        mine = total[:K] + total[K:]
        qbuf[s, var, :K] = mine
        if s == 0:
            qbuf[s, var, K:] = present_sum
            pl.semaphore_wait(barrier, S - 1 + V - 1)
        for d in range(1, V):
            q_copy(s, var, lax.rem(var + d, V)).start()
        for d in range(1, V):
            peer = lax.rem(var + d, V)
            q_copy(s, peer, peer).wait_recv()
        big = qbuf[s, 0, :K]
        for v in range(1, V):
            big = big + qbuf[s, v, :K]
        if s == 0:
            count = qbuf[0, 0, K:K + 8]
            for v in range(1, V):
                count = count + qbuf[0, v, K:K + 8]
            count = 1.0 / count[:1]
        mean = jnp.sum(f * big, axis=0, keepdims=True)
        f = f + f * ((big - mean) * count)

        f_t = fraction_rows(f)
        f_hi, f_lo = split2(f)
        left = jnp.concatenate([f_hi, f_lo], axis=0)
        for step in range(C):
            j = chunk(C - 1 - step)
            e = dot(f_t, pcat[j], 0)
            a = a_ref[j]
            b = b_ref[j]
            om = 1.0 - e
            inv = pl.reciprocal(e * om)
            ref_hi, ref_lo = split2(a * (om * inv))
            alt_hi, alt_lo = split2((b - a) * (e * inv))
            up = dot(left, ref_hi, 0) + dot(left, ref_lo, 0)
            low = dot(left, alt_hi, 0) + dot(left, alt_lo, 0)
            both = jnp.concatenate([up[:K] + up[K:], low[:K] + low[K:]], axis=0)
            psrc[s, j] = both

            @pl.when(j == mine_id)
            def _():
                precv[s, samp] = both

            @pl.when(j != mine_id)
            def _():
                p_copy(s, j, samp, first + j).start()

        @pl.when(owner)
        def _():
            for d in range(1, S):
                peer = lax.rem(samp + d, S)
                p_copy(s, 0, peer, peer).wait_recv()
            sums = precv[s, 0]
            for q in range(1, S):
                sums = sums + precv[s, q]
            old = fbuf[s, mine_id]
            upper = old * sums[:K]
            lower = (1.0 - old) * sums[K:]
            fbuf[s + 1, mine_id] = upper / (upper + lower)
            for d in range(1, S):
                g_copy(s, mine_id, lax.rem(samp + d, S)).start()

    out_f[...] = f
    for j in range(C):
        @pl.when(j != mine_id)
        def _():
            g_copy(ITERS - 1, j, j).wait_recv()
        out_p[:, j * W:(j + 1) * W] = fbuf[ITERS, j]

    for s in range(ITERS):
        for d in range(1, V):
            q_copy(s, var, lax.rem(var + d, V)).wait_send()
        for j in range(C):
            @pl.when(j != mine_id)
            def _():
                p_copy(s, j, samp, first + j).wait_send()

        @pl.when(owner)
        def _():
            for d in range(1, S):
                g_copy(s, mine_id, lax.rem(samp + d, S)).wait_send()


def shards(S, V, genotypes, ancestry, frequency):
    rows, cols = genotypes.shape
    K = ancestry.shape[0]
    C = 4
    W = cols // C
    dma = pltpu.SemaphoreType.DMA
    vmem = pl.BlockSpec(memory_space=pltpu.VMEM)
    return pl.pallas_call(
        functools.partial(kernel, S, V, C, W),
        out_shape=(
            jax.ShapeDtypeStruct(ancestry.shape, F32),
            jax.ShapeDtypeStruct(frequency.shape, F32),
        ),
        in_specs=[pl.BlockSpec(memory_space=pltpu.HBM)] * 3,
        out_specs=(vmem, vmem),
        scratch_shapes=[
            pltpu.VMEM((C, rows, W), jnp.int32),
            pltpu.VMEM((K, rows), F32),
            pltpu.VMEM((C, rows, W), F32),
            pltpu.VMEM((C, rows, W), F32),
            pltpu.VMEM((C, 8 * K, W), BF),
            pltpu.VMEM((ITERS + 1, C, K, W), F32),
            pltpu.VMEM((ITERS, V, K + 8, rows), F32),
            pltpu.VMEM((ITERS, C, 2 * K, W), F32),
            pltpu.VMEM((ITERS, S, 2 * K, W), F32),
            dma((C + 1,)), dma((C,)),
            dma((ITERS, V)), dma((ITERS, V)),
            dma((ITERS, C)), dma((ITERS, S)),
            dma((ITERS, S)), dma((ITERS, C)),
        ],
        compiler_params=pltpu.CompilerParams(
            collective_id=0, has_side_effects=True, vmem_limit_bytes=40 * 2 ** 20
        ),
        cost_estimate=pl.CostEstimate(
            flops=2 * 4 * 8 * rows * cols * K,
            bytes_accessed=4 * rows * cols,
            transcendentals=8 * rows * cols,
        ),
        name="em_sweeps",
    )(genotypes, ancestry, frequency)


def solution(mesh):
    return jax.shard_map(
        functools.partial(shards, mesh.shape["samp"], mesh.shape["var"]),
        mesh=mesh,
        in_specs=(P("samp", "var"), P(None, "samp"), P(None, "var")),
        out_specs=(P(None, "samp"), P(None, "var")),
        check_vma=False,
    )
```

```python
import functools

import jax
import jax.numpy as jnp
from jax import lax
from jax.experimental import pallas as pl
from jax.experimental.pallas import tpu as pltpu
from jax.sharding import PartitionSpec as P

ITERS = 4
Q_GROUPS = ((0,), (1,), (2,), (3,))
P_GROUPS = ((3,), (2,), (1,), (0,))
MESH = pl.DeviceIdType.MESH
BF = jnp.bfloat16
F32 = jnp.float32


def rounded(x):
    return x.astype(BF).astype(F32)


def split3(x):
    x1 = rounded(x)
    rest = x - x1
    x2 = rounded(rest)
    x3 = rounded(rest - x2)
    return x1, x2, x3


def split2(x):
    hi = x.astype(BF)
    return hi, (x - hi.astype(F32)).astype(BF)


def dot(left, right, right_dim):
    return lax.dot_general(
        left, right, (((1,), (right_dim,)), ((), ())), preferred_element_type=F32
    )


def kernel(
    S, V, C, W,
    geno_hbm, anc_hbm, freq_hbm, out_f, out_p,
    geno, anc, a_ref, b_ref, pcat, fbuf, qbuf, psrc, precv,
    in_sem, geno_sem, q_send, q_recv, p_send, p_recv, g_send, g_recv,
):
    K, rows = anc.shape
    samp = lax.axis_index("samp")
    var = lax.axis_index("var")
    first = (S - C) // 2
    mine_id = samp - first
    owner = jnp.logical_and(mine_id >= 0, mine_id < C)
    half = C // 2
    side, low_part = samp // (S // 2), lax.rem(samp, half)

    def chunk(step):
        return lax.rem(side + step // half, 2) * half + lax.rem(low_part + step % half, half)

    loads = [pltpu.make_async_copy(anc_hbm, anc, in_sem.at[C])]
    for j in range(C):
        loads.append(
            pltpu.make_async_copy(
                freq_hbm.at[:, pl.ds(j * W, W)], fbuf.at[0, j], in_sem.at[j]
            )
        )
    for load in loads:
        load.start()

    def geno_load(j):
        at = pl.ds(j * (rows // C), rows // C)
        return pltpu.make_async_copy(geno_hbm.at[at], geno.at[at], geno_sem.at[j])

    for step in range(C):
        geno_load(step).start()

    barrier = pltpu.get_barrier_semaphore()
    for d in range(1, S):
        pl.semaphore_signal(
            barrier, inc=1, device_id=(lax.rem(samp + d, S), var), device_id_type=MESH
        )
    for d in range(1, V):
        pl.semaphore_signal(
            barrier, inc=1, device_id=(samp, lax.rem(var + d, V)), device_id_type=MESH
        )

    def q_copy(s, slot, peer):
        return pltpu.make_async_remote_copy(
            src_ref=qbuf.at[s, slot], dst_ref=qbuf.at[s, slot],
            send_sem=q_send.at[s, peer], recv_sem=q_recv.at[s, slot],
            device_id=(samp, peer), device_id_type=MESH,
        )

    def p_copy(s, j, slot, peer):
        return pltpu.make_async_remote_copy(
            src_ref=psrc.at[s, j], dst_ref=precv.at[s, slot],
            send_sem=p_send.at[s, j], recv_sem=p_recv.at[s, slot],
            device_id=(peer, var), device_id_type=MESH,
        )

    def g_copy(s, slot, peer):
        return pltpu.make_async_remote_copy(
            src_ref=fbuf.at[s + 1, slot], dst_ref=fbuf.at[s + 1, slot],
            send_sem=g_send.at[s, peer], recv_sem=g_recv.at[s, slot],
            device_id=(peer, var), device_id_type=MESH,
        )

    def prepare(j):
        g = geno[:, pl.ds(pl.multiple_of(j * W, W), W)]
        present = g >= 0
        a_ref[j] = jnp.maximum(g, 0).astype(F32)
        b_ref[j] = jnp.where(present, 2.0, 0.0)

    def fraction_rows(f):
        f1, f2, f3 = split3(f)
        stacked = jnp.concatenate([f1, f1, f2, f2, f1, f3, f2, f3], axis=0)
        return jnp.transpose(stacked).astype(BF)

    for load in loads:
        load.wait()
    for step in range(C):
        geno_load(step).wait()
    f = anc[...]
    f = f / jnp.sum(f, axis=0, keepdims=True)
    count = None
    f_t = fraction_rows(f)
    for s in range(ITERS):
        total = jnp.zeros((2 * K, rows), F32)
        present_sum = jnp.zeros((8, rows), F32)
        for group in Q_GROUPS:
            chunks = [chunk(step) for step in group]
            for j in chunks:
                if s == 0:
                    prepare(j)
                else:

                    @pl.when(j != mine_id)
                    def _():
                        g_copy(s - 1, j, j).wait_recv()
            cats, diffs = [], []
            for j in chunks:
                p1, p2, p3 = split3(fbuf[s, j])
                cats.append(
                    jnp.concatenate([p1, p2, p1, p2, p3, p1, p3, p2], axis=0).astype(BF)
                )
            for j, cat in zip(chunks, cats):
                e = dot(f_t, cat, 0)
                diffs.append(
                    ((a_ref[j] - b_ref[j] * e) * pl.reciprocal(e * (1.0 - e))).astype(BF)
                )
            for j, cat, diff in zip(chunks, cats, diffs):
                left = cat[: 2 * K]
                total = total + dot(left, diff, 1)
                if s == 0:
                    present_sum = present_sum + dot(
                        jnp.ones((8, W), BF), b_ref[j].astype(BF), 1
                    )
            for j, cat in zip(chunks, cats):
                pcat[j] = cat
        mine = total[:K] + total[K:]
        qbuf[s, var, :K] = mine
        if s == 0:
            qbuf[s, var, K:] = present_sum
            pl.semaphore_wait(barrier, S - 1 + V - 1)
        for d in range(1, V):
            q_copy(s, var, lax.rem(var + d, V)).start()
        for d in range(1, V):
            peer = lax.rem(var + d, V)
            q_copy(s, peer, peer).wait_recv()
        big = qbuf[s, 0, :K]
        for v in range(1, V):
            big = big + qbuf[s, v, :K]
        if s == 0:
            count = qbuf[0, 0, K:K + 8]
            for v in range(1, V):
                count = count + qbuf[0, v, K:K + 8]
            count = 1.0 / count[:1]
        mean = jnp.sum(f * big, axis=0, keepdims=True)
        f = f + f * ((big - mean) * count)

        f_t = fraction_rows(f)
        f_hi, f_lo = split2(f)
        left = jnp.concatenate([f_hi, f_lo], axis=0)
        for group in P_GROUPS:
            chunks = [chunk(step) for step in group]
            ratios = []
            for j in chunks:
                e = dot(f_t, pcat[j], 0)
                a = a_ref[j]
                om = 1.0 - e
                inv = pl.reciprocal(e * om)
                ratios.append(
                    (split2(a * (om * inv)), split2((b_ref[j] - a) * (e * inv)))
                )
            sums = []
            for (ref_hi, ref_lo), (alt_hi, alt_lo) in ratios:
                up = dot(left, ref_hi, 0) + dot(left, ref_lo, 0)
                low = dot(left, alt_hi, 0) + dot(left, alt_lo, 0)
                sums.append(
                    jnp.concatenate([up[:K] + up[K:], low[:K] + low[K:]], axis=0)
                )
            for j, both in zip(chunks, sums):
                psrc[s, j] = both

                @pl.when(j == mine_id)
                def _():
                    precv[s, samp] = both

                @pl.when(j != mine_id)
                def _():
                    p_copy(s, j, samp, first + j).start()

        @pl.when(owner)
        def _():
            for d in range(1, S):
                peer = lax.rem(samp + d, S)
                p_copy(s, 0, peer, peer).wait_recv()
            sums = precv[s, 0]
            for q in range(1, S):
                sums = sums + precv[s, q]
            old = fbuf[s, mine_id]
            upper = old * sums[:K]
            lower = (1.0 - old) * sums[K:]
            fbuf[s + 1, mine_id] = upper / (upper + lower)
            for d in range(S - 1, 0, -1):
                g_copy(s, mine_id, lax.rem(samp + d, S)).start()

    out_f[...] = f
    for j in range(C):
        @pl.when(j != mine_id)
        def _():
            g_copy(ITERS - 1, j, j).wait_recv()
        out_p[:, j * W:(j + 1) * W] = fbuf[ITERS, j]

    for s in range(ITERS):
        for d in range(1, V):
            q_copy(s, var, lax.rem(var + d, V)).wait_send()
        for j in range(C):
            @pl.when(j != mine_id)
            def _():
                p_copy(s, j, samp, first + j).wait_send()

        @pl.when(owner)
        def _():
            for d in range(1, S):
                g_copy(s, mine_id, lax.rem(samp + d, S)).wait_send()


def shards(S, V, genotypes, ancestry, frequency):
    rows, cols = genotypes.shape
    K = ancestry.shape[0]
    C = 4
    W = cols // C
    dma = pltpu.SemaphoreType.DMA
    vmem = pl.BlockSpec(memory_space=pltpu.VMEM)
    return pl.pallas_call(
        functools.partial(kernel, S, V, C, W),
        out_shape=(
            jax.ShapeDtypeStruct(ancestry.shape, F32),
            jax.ShapeDtypeStruct(frequency.shape, F32),
        ),
        in_specs=[pl.BlockSpec(memory_space=pltpu.HBM)] * 3,
        out_specs=(vmem, vmem),
        scratch_shapes=[
            pltpu.VMEM((rows, cols), jnp.int32),
            pltpu.VMEM((K, rows), F32),
            pltpu.VMEM((C, rows, W), F32),
            pltpu.VMEM((C, rows, W), F32),
            pltpu.VMEM((C, 8 * K, W), BF),
            pltpu.VMEM((ITERS + 1, C, K, W), F32),
            pltpu.VMEM((ITERS, V, K + 8, rows), F32),
            pltpu.VMEM((ITERS, C, 2 * K, W), F32),
            pltpu.VMEM((ITERS, S, 2 * K, W), F32),
            dma((C + 1,)), dma((C,)),
            dma((ITERS, V)), dma((ITERS, V)),
            dma((ITERS, C)), dma((ITERS, S)),
            dma((ITERS, S)), dma((ITERS, C)),
        ],
        compiler_params=pltpu.CompilerParams(
            collective_id=0, has_side_effects=True, vmem_limit_bytes=40 * 2 ** 20
        ),
        cost_estimate=pl.CostEstimate(
            flops=2 * 4 * 8 * rows * cols * K,
            bytes_accessed=4 * rows * cols,
            transcendentals=8 * rows * cols,
        ),
        name="em_sweeps",
    )(genotypes, ancestry, frequency)


def solution(mesh):
    return jax.shard_map(
        functools.partial(shards, mesh.shape["samp"], mesh.shape["var"]),
        mesh=mesh,
        in_specs=(P("samp", "var"), P(None, "samp"), P(None, "var")),
        out_specs=(P(None, "samp"), P(None, "var")),
        check_vma=False,
    )
```
